256 devices in a mesh: prow: 32 (over y, z), pcol: 8 (over x, core).
Axes of the slice: x: 4, y: 4, z: 8, core: 2. Of those that a mesh axis runs over, the one named last changes fastest.
Arguments:
- trailing: bfloat16 [32768, 16384], P('prow', 'pcol'), may hold values from -6 to 6
- panel_block: bfloat16 [32768, 128], P('prow', 'pcol'), may hold values from -0.25 to 0.25
- lower_inverse: float32 [128, 128], replicated, as said below
- pivot_pairs: int32 [128], replicated, may hold values from 128 to 32767, as said below
Outputs:
- updated: bfloat16 [32768, 16384], P('prow', 'pcol')
The draws below stay inside these ranges and needn't reach their ends.
Inputs may be any that keep to these rules, and one draw needn't show every extreme that they name: `pivot_pairs`: the 128 values are distinct and all at least 128; both ends of the range occur. `lower_inverse`: unit lower triangular.
All inputs are finite; a program needn't handle non-finite values.
Results may differ from the reference program's by a relative error of at most 0.0043.
Values may be sent and summed in bfloat16 or wider, within the bound.
A program may use at most 64 MiB of HBM per device.

```python
import jax
import jax.numpy as jnp
from jax import lax

PANEL = 128
ROW_DEV = 1024
ROWS = 32768
COLS = 16384
N_PROW = 32


def draw_lower_inverse(key, part):
    key = jax.random.fold_in(key, 11)
    lower_part = jax.random.normal(key, (PANEL, PANEL), jnp.float32) * (0.6 / PANEL ** 0.5)
    return jnp.eye(PANEL, dtype=jnp.float32) + jnp.tril(lower_part, -1)


def draw_pivot_pairs(key, part):
    key = jax.random.fold_in(key, 23)
    first_key = jax.random.fold_in(key, 1)
    second_key = jax.random.fold_in(key, 2)
    interior = jax.random.permutation(first_key, ROWS - PANEL - 2).astype(jnp.int32) + (PANEL + 1)
    chosen = jnp.concatenate([jnp.array([PANEL], jnp.int32), interior[:PANEL - 2], jnp.array([ROWS - 1], jnp.int32)])
    shuffle = jax.random.permutation(second_key, PANEL)
    return chosen[shuffle].astype(jnp.int32)


def block_scale(own_key, shape, pieces, least, largest):
    loudness = 1.0
    for dim, parts in pieces:
        draws = jax.random.uniform(jax.random.fold_in(jax.random.fold_in(own_key, 6), dim), (parts,), jnp.float32, least / len(pieces), largest / len(pieces))
        loudness = loudness * jnp.repeat(jnp.exp(draws), shape[dim] // parts).reshape((-1,) + (1,) * (len(shape) - 1 - dim))
    return loudness


def centred(rng, dims, width, limit, cuts=(), held_as=jnp.bfloat16):
    result = jax.random.normal(rng, dims, jnp.float32) * width
    if len(cuts) > 0:
        result = block_scale(rng, dims, cuts, -0.22, 0.18) * result
    return jnp.clip(result, min=-limit, max=limit).astype(held_as)


def setup_inputs(seed: int = 0) -> dict:
    key_of = jax.random.split(jax.random.key(seed), 5)
    return {
        "trailing": centred(key_of[0], (ROWS, COLS), 1.0, 6.0, ((0, 32), (1, 8))),
        "panel_block": jnp.clip(jax.random.uniform(key_of[1], (ROWS, PANEL), jnp.float32, -0.25, 0.25) * block_scale(key_of[1], (ROWS, PANEL), ((0, 32), (1, 8)), -0.4, 0.0), -0.25, 0.25).astype(jnp.bfloat16),
        "lower_inverse": draw_lower_inverse(jax.random.fold_in(key_of[4], 71), 0),
        "pivot_pairs": draw_pivot_pairs(jax.random.fold_in(key_of[4], 71), 0),
    }


def to_global(stored):
    blocks = ROW_DEV // 128
    shaped = stored.reshape(N_PROW, blocks, 128, stored.shape[1])
    return shaped.transpose(1, 0, 2, 3).reshape(ROWS, stored.shape[1])


def to_stored(global_rows):
    blocks = ROW_DEV // 128
    shaped = global_rows.reshape(blocks, N_PROW, 128, global_rows.shape[1])
    return shaped.transpose(1, 0, 2, 3).reshape(ROWS, global_rows.shape[1])


def reference(trailing, panel_block, lower_inverse, pivot_pairs):
    global_rows = to_global(trailing)
    panel_global = to_global(panel_block)
    top_rows = global_rows[:PANEL]
    picked = global_rows[pivot_pairs]
    swapped = global_rows.at[pivot_pairs].set(top_rows)
    u_block = jnp.dot(lower_inverse, picked.astype(jnp.float32), precision=lax.Precision.HIGHEST).astype(jnp.bfloat16)
    product = jnp.dot(panel_global, u_block, preferred_element_type=jnp.float32)
    updated = (swapped.astype(jnp.float32) - product).astype(jnp.bfloat16)
    updated = updated.at[:PANEL].set(u_block)
    return to_stored(updated)
```

```python
import functools

import jax
import jax.numpy as jnp
from jax import lax
from jax.experimental import pallas as pl
from jax.experimental.pallas import tpu as pltpu
from jax.sharding import PartitionSpec as P

MESH = pl.DeviceIdType.MESH
LANES = 128


def torus_of(procs):
    n_y = {32: 4, 8: 2}[procs]
    return n_y, procs // n_y


def near_first(n):
    return sorted(range(1, n), key=lambda k: (min(k, n - k), k))


def far_first(n):
    return sorted(range(n), key=lambda k: (-min(k, n - k), k))


def kernel(n_y, n_z, n_c, rows, cols, width,
           trailing_ref, panel_ref, inverse_ref, pivots_ref, out_ref,
           held, picked, from_y, summed, from_z, pieces, top_out, top_in, panels, left,
           panel_held, inverse_held, pivots_held, small_sem, load_sem, ry_send, ry_recv, rz_send, rz_recv, top_send, top_recv, spread_send, spread_recv,
           gz_send, gz_recv, gy_send, gy_recv, panel_send, panel_recv):
    procs = n_y * n_z
    n_j = n_z // 2
    half = width // 2
    group = cols // n_y
    me = lax.axis_index("prow")
    c = lax.axis_index("pcol")
    y, z = me // n_z, me % n_z
    j_own, h_own = z // 2, z % 2
    is_root = me == 0

    def y_peer(k):
        return (y + k) % n_y

    def z_peer(k):
        return (z + k) % n_z

    def send(src, dst, send_sem, recv_sem, row, col):
        copy = pltpu.make_async_remote_copy(
            src_ref=src, dst_ref=dst, send_sem=send_sem, recv_sem=recv_sem,
            device_id=(row, col), device_id_type=MESH,
        )
        copy.start()
        return copy

    def arrived(dst, recv_sem):
        pltpu.make_async_remote_copy(
            src_ref=dst, dst_ref=dst, send_sem=recv_sem, recv_sem=recv_sem,
            device_id=(me, c), device_id_type=MESH,
        ).wait_recv()

    barrier = pltpu.get_barrier_semaphore()
    for k in range(1, n_y):
        pl.semaphore_signal(barrier, inc=1, device_id=(y_peer(k) * n_z + z, c), device_id_type=MESH)
    for k in range(1, n_z):
        pl.semaphore_signal(barrier, inc=1, device_id=(y * n_z + z_peer(k), c), device_id_type=MESH)
    for k in range(1, n_c):
        pl.semaphore_signal(barrier, inc=1, device_id=(me, (c + k) % n_c), device_id_type=MESH)

    small = [
        pltpu.make_async_copy(pivots_ref, pivots_held, small_sem.at[0]),
        pltpu.make_async_copy(panel_ref, panel_held, small_sem.at[1]),
        pltpu.make_async_copy(inverse_ref, inverse_held, small_sem.at[2]),
    ]
    for copy in small:
        copy.start()

    y_order = list(range(1, n_y)) + [0]
    loads = []
    for k in y_order:
        span = pl.ds(pl.multiple_of(y_peer(k) * group, group), group)
        load = pltpu.make_async_copy(trailing_ref.at[:, span], held.at[:, span], load_sem.at[k])
        load.start()
        loads.append(load)

    small[0].wait()
    pivots = pivots_held[...]
    block = pivots // width
    where = jnp.where(block % procs == me, block // procs * width + pivots % width, -1)
    where = where.astype(jnp.float32)
    spread = jnp.broadcast_to(where, (width, width)).T
    for b in range(rows // LANES):
        row = lax.broadcasted_iota(jnp.int32, (width, LANES), 1) + b * LANES
        select = (spread == row.astype(jnp.float32)).astype(jnp.bfloat16)
        left[width:2 * width, b * LANES:(b + 1) * LANES] = select

    for n, k in enumerate(y_order):
        loads[n].wait()
        yk = y_peer(k)
        span = pl.ds(pl.multiple_of(yk * group, group), group)
        rows_out = jnp.dot(left[width:2 * width, :], held[:, span], preferred_element_type=jnp.float32)
        rows_out = rows_out.astype(jnp.bfloat16)
        for j in range(n_j):
            picked[yk, j] = rows_out[:, j * LANES:(j + 1) * LANES]

    @pl.when(is_root)
    def _():
        for k in range(n_z):
            for q in range(n_y):
                at = (q * n_j + k // 2) * LANES
                top_out[k, q] = held[(k % 2) * half:(k % 2 + 1) * half, at:at + LANES]

    pl.semaphore_wait(barrier, n_y - 1 + n_z - 1 + n_c - 1)

    @pl.when(is_root)
    def _():
        copies = []
        for k in range(1, n_z):
            copies.append(send(top_out.at[k], top_in, top_send.at[k], top_recv.at[0], k, c))
        top_in[...] = top_out[0]

    j_order = [m for m in far_first(n_j)]
    ry_copies = []
    for m in j_order:
        j = (j_own + m) % n_j
        for k in range(1, n_y):
            yk = y_peer(k)
            ry_copies.append(send(picked.at[yk, j], from_y.at[j, k], ry_send.at[m, k], ry_recv.at[j, k],
                                  yk * n_z + z, c))

    small[1].wait()
    panel_copies = []
    for k in range(1, n_c):
        ck = (c + k) % n_c
        panel_copies.append(send(panel_held, panels.at[c], panel_send.at[k], panel_recv.at[k], me, ck))
    panels[c] = panel_held[...]

    rz_copies = []
    for m in j_order:
        j = (j_own + m) % n_j
        for k in range(1, n_y):
            arrived(from_y.at[j, k], ry_recv.at[j, k])
        total = picked[y, j]
        for k in range(1, n_y):
            total = total + from_y[j, k]
        summed[j] = total
        if m == 0:
            zk = j * 2 + 1 - h_own
            rz_copies.append(send(summed.at[j], from_z.at[z], rz_send.at[0], rz_recv.at[z], y * n_z + zk, c))
        else:
            for h in range(2):
                zk = j * 2 + h
                rz_copies.append(send(summed.at[j], from_z.at[z], rz_send.at[m * 2 + h], rz_recv.at[z],
                                      y * n_z + zk, c))

    @pl.when(y == 0)
    def _():
        @pl.when(z != 0)
        def _():
            arrived(top_in, top_recv.at[0])
        for k in range(1, n_y):
            send(top_in.at[k], pieces.at[k * n_z + z, 1], spread_send.at[k], spread_recv.at[0], k * n_z + z, c)
        pieces[me, 1] = top_in[0]

    for k in range(1, n_c):
        ck = (c + n_c - k) % n_c
        arrived(panels.at[ck], panel_recv.at[k])
    share = width // n_c
    for k in range(n_c):
        left[k * share:(k + 1) * share, :] = -panels[k]

    @pl.when(is_root)
    def _():
        row = lax.broadcasted_iota(jnp.int32, (width, width), 0)
        col = lax.broadcasted_iota(jnp.int32, (width, width), 1)
        left[0:width, 0:width] = (row == col).astype(jnp.bfloat16)

    tile = LANES

    def mask(b, carry):
        span = pl.ds(pl.multiple_of(b * tile, tile), tile)
        hit = jnp.sum(left[width:2 * width, span].astype(jnp.float32), axis=0, keepdims=True)
        hit = jnp.where(jnp.logical_and(is_root, b == 0), 1.0, hit)
        keep = (1.0 - jnp.broadcast_to(hit, (tile, tile))).T
        keep = keep.astype(jnp.bfloat16)
        for g in range(cols // LANES):
            part = pl.ds(g * LANES, LANES)
            held[span, part] = held[span, part] * keep
        return carry

    lax.fori_loop(0, rows // tile, mask, 0)

    total = summed[j_own]
    for k in near_first(n_z):
        zk = z_peer(k)
        arrived(from_z.at[zk], rz_recv.at[zk])
        total = total + from_z[zk]
    small[2].wait()
    inverse = inverse_held[pl.ds(pl.multiple_of(h_own * half, half), half), :]
    u = jnp.dot(inverse, total.astype(jnp.float32), precision=lax.Precision.HIGHEST,
                preferred_element_type=jnp.float32)
    pieces[me, 0] = u.astype(jnp.bfloat16)

    @pl.when(y != 0)
    def _():
        arrived(pieces.at[me, 1], spread_recv.at[0])

    gz_copies, gy_copies = [], []
    for k in near_first(n_z)[::-1]:
        gz_copies.append(send(pieces.at[me], pieces.at[me], gz_send.at[k], gz_recv.at[z], y * n_z + z_peer(k), c))
    for kz in [0] + near_first(n_z):
        zk = z_peer(kz)
        slot = y * n_z + zk
        if kz:
            arrived(pieces.at[slot], gz_recv.at[zk])
        for k in range(1, n_y):
            gy_copies.append(send(pieces.at[slot], pieces.at[slot], gy_send.at[kz, k], gy_recv.at[slot],
                                  y_peer(k) * n_z + z, c))

    for k in range(n_y):
        yk = y_peer(k)
        for pair in range(n_j // 2):
            base = yk * n_z + pair * 4
            if k:
                for q in range(4):
                    arrived(pieces.at[base + q], gy_recv.at[base + q])
            right = jnp.concatenate([
                jnp.concatenate([pieces[base + 0, part], pieces[base + 1, part]], axis=0)
                for part in range(2)
            ], axis=0)
            right_2 = jnp.concatenate([
                jnp.concatenate([pieces[base + 2, part], pieces[base + 3, part]], axis=0)
                for part in range(2)
            ], axis=0)
            right = jnp.concatenate([right, right_2], axis=1)
            span = pl.ds(pl.multiple_of((yk * n_j + pair * 2) * LANES, 2 * LANES), 2 * LANES)
            term = lax.dot_general(left[...], right, (((0,), (0,)), ((), ())),
                                   preferred_element_type=jnp.float32)
            out_ref[:, span] = (held[:, span].astype(jnp.float32) + term).astype(jnp.bfloat16)

    for copy in ry_copies + panel_copies + rz_copies + gz_copies + gy_copies:
        copy.wait_send()

    @pl.when(is_root)
    def _():
        for k in range(1, n_z):
            pltpu.make_async_remote_copy(
                src_ref=top_out.at[k], dst_ref=top_in, send_sem=top_send.at[k], recv_sem=top_recv.at[0],
                device_id=(k, c), device_id_type=MESH).wait_send()

    @pl.when(y == 0)
    def _():
        for k in range(1, n_y):
            pltpu.make_async_remote_copy(
                src_ref=top_in.at[k], dst_ref=pieces.at[k * n_z + z, 1], send_sem=spread_send.at[k],
                recv_sem=spread_recv.at[0], device_id=(k * n_z + z, c), device_id_type=MESH).wait_send()


def shards(trailing, panel_block, lower_inverse, pivot_pairs):
    rows, cols = trailing.shape
    width = lower_inverse.shape[0]
    procs, n_c = lax.axis_size("prow"), lax.axis_size("pcol")
    n_y, n_z = torus_of(procs)
    n_j, half, share = n_z // 2, width // 2, width // n_c
    bf16 = jnp.bfloat16
    dma = pltpu.SemaphoreType.DMA
    vmem = pl.BlockSpec(memory_space=pltpu.VMEM)
    return pl.pallas_call(
        functools.partial(kernel, n_y, n_z, n_c, rows, cols, width),
        out_shape=pltpu.VMEM((rows, cols), bf16),
        in_specs=[pl.BlockSpec(memory_space=pltpu.HBM)] * 4,
        out_specs=vmem,
        scratch_shapes=[
            pltpu.VMEM((rows, cols), bf16),
            pltpu.VMEM((n_y, n_j, width, LANES), bf16),
            pltpu.VMEM((n_j, n_y, width, LANES), bf16),
            pltpu.VMEM((n_j, width, LANES), bf16),
            pltpu.VMEM((n_z, width, LANES), bf16),
            pltpu.VMEM((procs, 2, half, LANES), bf16),
            pltpu.VMEM((n_z, n_y, half, LANES), bf16),
            pltpu.VMEM((n_y, half, LANES), bf16),
            pltpu.VMEM((n_c, share, rows), bf16),
            pltpu.VMEM((2 * width, rows), bf16),
            pltpu.VMEM((share, rows), bf16),
            pltpu.VMEM((width, width), jnp.float32),
            pltpu.VMEM((1, width), jnp.int32),
            dma((3,)), dma((n_y,)), dma((n_j, n_y)), dma((n_j, n_y)), dma((n_z,)), dma((n_z,)),
            dma((n_z,)), dma((1,)), dma((n_y,)), dma((1,)),
            dma((n_z,)), dma((n_z,)), dma((n_z, n_y)), dma((procs,)), dma((n_c,)), dma((n_c,)),
        ],
        compiler_params=pltpu.CompilerParams(
            collective_id=0, has_side_effects=True, vmem_limit_bytes=32 * 1024 * 1024
        ),
        name="lu_update",
    )(*(
        pltpu.with_memory_space_constraint(value, pltpu.HBM)
        for value in (trailing, panel_block.T, lower_inverse, pivot_pairs.reshape(1, width))
    ))


def solution(mesh):
    in_specs = (P("prow", "pcol"), P("prow", "pcol"), P(), P())
    out_specs = P("prow", "pcol")
    return jax.shard_map(shards, mesh=mesh, in_specs=in_specs, out_specs=out_specs, check_vma=False)
```

```python
import functools

import jax
import jax.numpy as jnp
from jax import lax
from jax.experimental import pallas as pl
from jax.experimental.pallas import tpu as pltpu
from jax.sharding import PartitionSpec as P

MESH = pl.DeviceIdType.MESH
LANES = 128


def torus_of(procs):
    n_y = {32: 4, 8: 2}[procs]
    return n_y, procs // n_y


def near_first(n):
    return sorted(range(1, n), key=lambda k: (min(k, n - k), k))


def far_first(n):
    return sorted(range(n), key=lambda k: (-min(k, n - k), k))


def kernel(n_y, n_z, n_c, rows, cols, width,
           trailing_ref, panel_ref, inverse_ref, pivots_ref, held, left, right,
           select, picked, from_y, summed, from_z, u_all, top_all, top_out, top_in, panels,
           panel_held, inverse_held, pivots_held,
           small_sem, load_sem, ry_send, ry_recv, rz_send, rz_recv, top_send, top_recv, spread_send, spread_recv,
           uz_send, uz_recv, uy_send, uy_recv, tz_send, tz_recv, ty_send, ty_recv, panel_send, panel_recv):
    procs = n_y * n_z
    n_j = n_z // 2
    half = width // 2
    group = cols // n_y
    share = width // n_c
    me = lax.axis_index("prow")
    c = lax.axis_index("pcol")
    y, z = me // n_z, me % n_z
    j_own, h_own = z // 2, z % 2
    is_root = me == 0
    bf16 = jnp.bfloat16

    def y_peer(k):
        return (y + k) % n_y

    def z_peer(k):
        return (z + k) % n_z

    def remote(src, dst, send_sem, recv_sem, row, col):
        return pltpu.make_async_remote_copy(
            src_ref=src, dst_ref=dst, send_sem=send_sem, recv_sem=recv_sem,
            device_id=(row, col), device_id_type=MESH,
        )

    sent = []

    def send(*what):
        copy = remote(*what)
        copy.start()
        sent.append(copy)

    def arrived(dst, recv_sem):
        remote(dst, dst, recv_sem, recv_sem, me, c).wait_recv()

    barrier = pltpu.get_barrier_semaphore()
    for k in far_first(n_z)[:-1]:
        pl.semaphore_signal(barrier, inc=1, device_id=(y * n_z + z_peer(k), c), device_id_type=MESH)
    for k in far_first(n_y)[:-1]:
        pl.semaphore_signal(barrier, inc=1, device_id=(y_peer(k) * n_z + z, c), device_id_type=MESH)
    for k in range(1, n_c):
        pl.semaphore_signal(barrier, inc=1, device_id=(me, (c + k) % n_c), device_id_type=MESH)

    small = [
        pltpu.make_async_copy(pivots_ref, pivots_held, small_sem.at[0]),
        pltpu.make_async_copy(panel_ref, panel_held, small_sem.at[1]),
        pltpu.make_async_copy(inverse_ref, inverse_held, small_sem.at[2]),
    ]
    small[0].start()

    y_order = far_first(n_y)
    loads = []
    for k in y_order:
        span = pl.ds(pl.multiple_of(y_peer(k) * group, group), group)
        load = pltpu.make_async_copy(trailing_ref.at[:, span], held.at[:, span], load_sem.at[k])
        load.start()
        loads.append(load)
    small[1].start()
    small[2].start()

    small[0].wait()
    pivots = pivots_held[...]
    block = pivots // width
    where = jnp.where(block % procs == me, block // procs * width + pivots % width, -1)
    spread = jnp.broadcast_to(where.astype(jnp.float32), (width, width)).T
    for b in range(rows // LANES):
        row = lax.broadcasted_iota(jnp.int32, (width, LANES), 1) + b * LANES
        select[:, b * LANES:(b + 1) * LANES] = (spread == row.astype(jnp.float32)).astype(bf16)

    j_order = far_first(n_j)
    for n, k in enumerate(y_order):
        loads[n].wait()
        yk = y_peer(k)
        span = pl.ds(pl.multiple_of(yk * group, group), group)
        found = jnp.dot(select[...], held[:, span], preferred_element_type=jnp.float32).astype(bf16)
        for j in range(n_j):
            picked[yk, j] = found[:, j * LANES:(j + 1) * LANES]

    @pl.when(is_root)
    def _():
        for k in far_first(n_z):
            for q in range(n_y):
                at = (q * n_j + k // 2) * LANES
                top_out[k, q] = held[(k % 2) * half:(k % 2 + 1) * half, at:at + LANES]
        top_in[...] = top_out[0]

    pl.semaphore_wait(barrier, n_y - 1 + n_z - 1 + n_c - 1)

    @pl.when(is_root)
    def _():
        for k in far_first(n_z)[:-1]:
            remote(top_out.at[k], top_in, top_send.at[k], top_recv.at[0], k, c).start()

    for m in j_order:
        j = (j_own + m) % n_j
        for k in far_first(n_y)[:-1]:
            yk = y_peer(k)
            send(picked.at[yk, j], from_y.at[j, k], ry_send.at[m, k], ry_recv.at[j, k], yk * n_z + z, c)

    small[1].wait()
    for k in range(1, n_c):
        ck = (c + k) % n_c
        send(panel_held, panels.at[c], panel_send.at[k], panel_recv.at[k], me, ck)
    panels[c] = panel_held[...]

    def spread_z(ref, send_sems, recv_sems):
        for k in near_first(n_z):
            send(ref.at[me], ref.at[me], send_sems.at[k], recv_sems.at[z], y * n_z + z_peer(k), c)

    def hand_on(ref, send_sems, recv_sems, kz):
        slot = y * n_z + z_peer(kz)
        for k in far_first(n_y)[:-1]:
            send(ref.at[slot], ref.at[slot], send_sems.at[kz, k], recv_sems.at[slot], y_peer(k) * n_z + z, c)

    def hand_on_all(ref, z_sems, send_sems, recv_sems):
        for kz in near_first(n_z):
            zk = z_peer(kz)
            arrived(ref.at[y * n_z + zk], z_sems.at[zk])
            hand_on(ref, send_sems, recv_sems, kz)

    def top_along_y():
        @pl.when(y == 0)
        def _():
            @pl.when(z != 0)
            def _():
                arrived(top_in, top_recv.at[0])
            for k in far_first(n_y)[:-1]:
                remote(top_in.at[k], top_all.at[k * n_z + z], spread_send.at[k], spread_recv.at[0],
                       k * n_z + z, c).start()
            top_all[me] = top_in[0]

    for m in j_order:
        j = (j_own + m) % n_j
        for k in range(1, n_y):
            arrived(from_y.at[j, k], ry_recv.at[j, k])
        total = picked[y, j]
        for k in range(1, n_y):
            total = total + from_y[j, k]
        summed[j] = total
        for h in range(2) if m else range(1):
            zk = j * 2 + h if m else j * 2 + 1 - h_own
            send(summed.at[j], from_z.at[z], rz_send.at[m * 2 + h], rz_recv.at[z], y * n_z + zk, c)
        if m == j_order[1]:
            top_along_y()

    tile = LANES

    def mask(b, carry):
        span = pl.ds(pl.multiple_of(b * tile, tile), tile)
        row = lax.broadcasted_iota(jnp.int32, (tile, width), 0) + b * tile
        hit = (where == row).astype(jnp.float32)
        left[span, width:2 * width] = hit.astype(bf16)
        hit = jnp.sum(hit, axis=1, keepdims=True)
        hit = jnp.where(jnp.logical_and(is_root, b == 0), 1.0, hit)
        keep = jnp.broadcast_to(1.0 - hit, (tile, LANES)).astype(bf16)
        for g in range(cols // LANES):
            part = pl.ds(g * LANES, LANES)
            held[span, part] = held[span, part] * keep
        return carry

    lax.fori_loop(0, rows // tile, mask, 0)

    @pl.when(y != 0)
    def _():
        arrived(top_all.at[me], spread_recv.at[0])

    spread_z(top_all, tz_send, tz_recv)
    hand_on(top_all, ty_send, ty_recv, 0)

    small[2].wait()
    inverse = inverse_held[pl.ds(pl.multiple_of(h_own * half, half), half), :]
    total = summed[j_own]
    for k in near_first(n_z):
        zk = z_peer(k)
        arrived(from_z.at[zk], rz_recv.at[zk])
        total = total + from_z[zk]
    u = jnp.dot(inverse, total.astype(jnp.float32), precision=lax.Precision.HIGHEST,
                preferred_element_type=jnp.float32)
    u_all[me] = u.astype(bf16)

    spread_z(u_all, uz_send, uz_recv)
    hand_on(u_all, uy_send, uy_recv, 0)
    hand_on_all(top_all, tz_recv, ty_send, ty_recv)

    for k in range(1, n_c):
        arrived(panels.at[(c + n_c - k) % n_c], panel_recv.at[k])
    whole = jnp.concatenate([panels[k] for k in range(n_c)], axis=0)
    left[:, 0:width] = -whole.astype(jnp.float32).T.astype(bf16)

    @pl.when(is_root)
    def _():
        row = lax.broadcasted_iota(jnp.int32, (width, width), 0)
        col = lax.broadcasted_iota(jnp.int32, (width, width), 1)
        left[0:width, 0:width] = (row == col).astype(bf16)

    hand_on_all(u_all, uz_recv, uy_send, uy_recv)

    for k in range(n_y):
        yk = y_peer(k)
        for j in range(n_j):
            span = pl.ds(pl.multiple_of((yk * n_j + j) * LANES, LANES), LANES)
            for h in range(2):
                slot = yk * n_z + j * 2 + h
                if k:
                    arrived(top_all.at[slot], ty_recv.at[slot])
                right[width + h * half:width + (h + 1) * half, span] = top_all[slot]
    for k in range(n_y):
        yk = y_peer(k)
        for j in range(n_j):
            span = pl.ds(pl.multiple_of((yk * n_j + j) * LANES, LANES), LANES)
            for h in range(2):
                slot = yk * n_z + j * 2 + h
                if k:
                    arrived(u_all.at[slot], uy_recv.at[slot])
                right[h * half:(h + 1) * half, span] = u_all[slot]

    for copy in sent:
        copy.wait_send()

    @pl.when(is_root)
    def _():
        for k in range(1, n_z):
            remote(top_out.at[k], top_in, top_send.at[k], top_recv.at[0], k, c).wait_send()

    @pl.when(y == 0)
    def _():
        for k in range(1, n_y):
            remote(top_in.at[k], top_all.at[k * n_z + z], spread_send.at[k], spread_recv.at[0],
                   k * n_z + z, c).wait_send()


def update(parts, held, left, right, out_ref, done, sems):
    step = held.shape[1] // parts
    for n in range(parts):
        span = slice(n * step, (n + 1) * step)
        term = jnp.dot(left[...], right[:, span], preferred_element_type=jnp.float32)
        done[n] = (held[:, span].astype(jnp.float32) + term).astype(jnp.bfloat16)
        pltpu.make_async_copy(done.at[n], out_ref.at[:, span], sems.at[n]).start()
    for n in range(parts):
        span = slice(n * step, (n + 1) * step)
        pltpu.make_async_copy(done.at[n], out_ref.at[:, span], sems.at[n]).wait()


def shards(trailing, panel_block, lower_inverse, pivot_pairs):
    rows, cols = trailing.shape
    width = lower_inverse.shape[0]
    procs, n_c = lax.axis_size("prow"), lax.axis_size("pcol")
    n_y, n_z = torus_of(procs)
    n_j, half, share = n_z // 2, width // 2, width // n_c
    bf16 = jnp.bfloat16
    dma = pltpu.SemaphoreType.DMA
    vmem = pl.BlockSpec(memory_space=pltpu.VMEM)
    factors = pl.pallas_call(
        functools.partial(kernel, n_y, n_z, n_c, rows, cols, width),
        out_shape=[
            pltpu.VMEM((rows, cols), bf16), pltpu.VMEM((rows, 2 * width), bf16), pltpu.VMEM((2 * width, cols), bf16)
        ],
        in_specs=[pl.BlockSpec(memory_space=pltpu.HBM)] * 4,
        out_specs=[vmem] * 3,
        scratch_shapes=[
            pltpu.VMEM((width, rows), bf16),
            pltpu.VMEM((n_y, n_j, width, LANES), bf16),
            pltpu.VMEM((n_j, n_y, width, LANES), bf16),
            pltpu.VMEM((n_j, width, LANES), bf16),
            pltpu.VMEM((n_z, width, LANES), bf16),
            pltpu.VMEM((procs, half, LANES), bf16),
            pltpu.VMEM((procs, half, LANES), bf16),
            pltpu.VMEM((n_z, n_y, half, LANES), bf16),
            pltpu.VMEM((n_y, half, LANES), bf16),
            pltpu.VMEM((n_c, share, rows), bf16),
            pltpu.VMEM((share, rows), bf16),
            pltpu.VMEM((width, width), jnp.float32),
            pltpu.VMEM((1, width), jnp.int32),
            dma((3,)), dma((n_y,)), dma((n_j, n_y)), dma((n_j, n_y)), dma((n_z,)), dma((n_z,)),
            dma((n_z,)), dma((1,)), dma((n_y,)), dma((1,)),
            dma((n_z,)), dma((n_z,)), dma((n_z, n_y)), dma((procs,)),
            dma((n_z,)), dma((n_z,)), dma((n_z, n_y)), dma((procs,)), dma((n_c,)), dma((n_c,)),
        ],
        compiler_params=pltpu.CompilerParams(
            collective_id=0, has_side_effects=True, vmem_limit_bytes=32 * 1024 * 1024
        ),
        name="exchange",
    )(*(
        pltpu.with_memory_space_constraint(value, pltpu.HBM)
        for value in (trailing, panel_block.T, lower_inverse, pivot_pairs.reshape(1, width))
    ))
    parts = cols // (2 * LANES)
    return pl.pallas_call(
        functools.partial(update, parts),
        out_shape=jax.ShapeDtypeStruct((rows, cols), bf16),
        in_specs=[vmem] * 3,
        out_specs=pl.BlockSpec(memory_space=pltpu.HBM),
        scratch_shapes=[pltpu.VMEM((parts, rows, cols // parts), bf16), dma((parts,))],
        compiler_params=pltpu.CompilerParams(vmem_limit_bytes=32 * 1024 * 1024),
        name="update",
    )(*(pltpu.with_memory_space_constraint(value, pltpu.VMEM) for value in factors))


def solution(mesh):
    in_specs = (P("prow", "pcol"), P("prow", "pcol"), P(), P())
    out_specs = P("prow", "pcol")
    return jax.shard_map(shards, mesh=mesh, in_specs=in_specs, out_specs=out_specs, check_vma=False)
```

```python
import functools

import jax
import jax.numpy as jnp
from jax import lax
from jax.experimental import pallas as pl
from jax.experimental.pallas import tpu as pltpu
from jax.sharding import PartitionSpec as P

MESH = pl.DeviceIdType.MESH
LANES = 128


def torus_of(procs):
    n_y = {32: 4, 8: 2}[procs]
    return n_y, procs // n_y


def near_first(n):
    return sorted(range(1, n), key=lambda k: (min(k, n - k), k))


def far_first(n):
    return sorted(range(n), key=lambda k: (-min(k, n - k), k))


def kernel(n_y, n_z, n_c, rows, cols, width,
           trailing_ref, panel_ref, inverse_ref, pivots_ref, held, left, right,
           select, picked, from_y, summed, from_z, u_all, top_all, top_out, top_in, panels,
           panel_held, inverse_held, pivots_held,
           small_sem, load_sem, ry_send, ry_recv, rz_send, rz_recv, top_send, top_recv, spread_send, spread_recv,
           uz_send, uz_recv, uy_send, uy_recv, tz_send, tz_recv, ty_send, ty_recv, panel_send, panel_recv):
    procs = n_y * n_z
    n_j = n_z // 2
    group = cols // n_y
    share = width // n_c
    me = lax.axis_index("prow")
    c = lax.axis_index("pcol")
    y, z = me // n_z, me % n_z
    j_own, collects = z // 2, z % 2 == 0
    mine = y * n_j + j_own
    is_root = me == 0
    bf16 = jnp.bfloat16

    def y_peer(k):
        return (y + k) % n_y

    def z_peer(k):
        return (z + k) % n_z

    def remote(src, dst, send_sem, recv_sem, row, col):
        return pltpu.make_async_remote_copy(
            src_ref=src, dst_ref=dst, send_sem=send_sem, recv_sem=recv_sem,
            device_id=(row, col), device_id_type=MESH,
        )

    sent = []

    def send(*what):
        copy = remote(*what)
        copy.start()
        sent.append(copy)

    def arrived(dst, recv_sem):
        remote(dst, dst, recv_sem, recv_sem, me, c).wait_recv()

    barrier = pltpu.get_barrier_semaphore()
    for k in far_first(n_z)[:-1]:
        pl.semaphore_signal(barrier, inc=1, device_id=(y * n_z + z_peer(k), c), device_id_type=MESH)
    for k in far_first(n_y)[:-1]:
        pl.semaphore_signal(barrier, inc=1, device_id=(y_peer(k) * n_z + z, c), device_id_type=MESH)
    for k in range(1, n_c):
        pl.semaphore_signal(barrier, inc=1, device_id=(me, (c + k) % n_c), device_id_type=MESH)

    small = [
        pltpu.make_async_copy(pivots_ref, pivots_held, small_sem.at[0]),
        pltpu.make_async_copy(panel_ref, panel_held, small_sem.at[1]),
        pltpu.make_async_copy(inverse_ref, inverse_held, small_sem.at[2]),
    ]
    small[0].start()

    y_order = far_first(n_y)
    loads = []
    for k in y_order:
        span = pl.ds(pl.multiple_of(y_peer(k) * group, group), group)
        load = pltpu.make_async_copy(trailing_ref.at[:, span], held.at[:, span], load_sem.at[k])
        load.start()
        loads.append(load)
    small[1].start()
    small[2].start()

    small[0].wait()
    pivots = pivots_held[...]
    block = pivots // width
    where = jnp.where(block % procs == me, block // procs * width + pivots % width, -1)
    spread = jnp.broadcast_to(where.astype(jnp.float32), (width, width)).T
    for b in range(rows // LANES):
        row = lax.broadcasted_iota(jnp.int32, (width, LANES), 1) + b * LANES
        select[:, b * LANES:(b + 1) * LANES] = (spread == row.astype(jnp.float32)).astype(bf16)

    j_order = far_first(n_j)
    for n, k in enumerate(y_order):
        loads[n].wait()
        yk = y_peer(k)
        span = pl.ds(pl.multiple_of(yk * group, group), group)
        found = jnp.dot(select[...], held[:, span], preferred_element_type=jnp.float32).astype(bf16)
        for j in range(n_j):
            picked[yk, j] = found[:, j * LANES:(j + 1) * LANES]

    @pl.when(is_root)
    def _():
        for j in far_first(n_j):
            for q in range(n_y):
                at = (q * n_j + j) * LANES
                top_out[j, q] = held[0:width, at:at + LANES]
        top_in[...] = top_out[0]

    pl.semaphore_wait(barrier, n_y - 1 + n_z - 1 + n_c - 1)

    def top_along_z(j):
        return remote(top_out.at[j], top_in, top_send.at[j], top_recv.at[0], j * 2, c)

    @pl.when(is_root)
    def _():
        for j in far_first(n_j)[:-1]:
            top_along_z(j).start()

    for m in j_order:
        j = (j_own + m) % n_j
        for k in far_first(n_y)[:-1]:
            yk = y_peer(k)
            send(picked.at[yk, j], from_y.at[j, k], ry_send.at[m, k], ry_recv.at[j, k], yk * n_z + z, c)

    small[1].wait()
    for k in range(1, n_c):
        ck = (c + k) % n_c
        send(panel_held, panels.at[c], panel_send.at[k], panel_recv.at[k], me, ck)
    panels[c] = panel_held[...]

    def spread_z(ref, send_sems, recv_sems):
        for k in near_first(n_z):
            send(ref.at[me], ref.at[me], send_sems.at[k], recv_sems.at[z], y * n_z + z_peer(k), c)

    def hand_on(ref, send_sems, recv_sems, kz):
        slot = y * n_z + z_peer(kz)
        for k in far_first(n_y)[:-1]:
            send(ref.at[slot], ref.at[slot], send_sems.at[kz, k], recv_sems.at[slot], y_peer(k) * n_z + z, c)

    def hand_on_all(ref, z_sems, send_sems, recv_sems):
        for kz in near_first(n_z):
            zk = z_peer(kz)
            arrived(ref.at[y * n_z + zk], z_sems.at[zk])
            hand_on(ref, send_sems, recv_sems, kz)

    def top_along_y(k):
        return remote(top_in.at[k], top_all.at[k * n_j + j_own], spread_send.at[k], spread_recv.at[0],
                      k * n_z + z, c)

    def pass_top_on():
        @pl.when(z != 0)
        def _():
            arrived(top_in, top_recv.at[0])
        for k in far_first(n_y)[:-1]:
            top_along_y(k).start()
        top_all[mine] = top_in[0]

    def to_collector(m):
        j = (j_own + m) % n_j
        return remote(summed.at[j], from_z.at[z], rz_send.at[m], rz_recv.at[z], y * n_z + j * 2, c)

    for m in j_order:
        j = (j_own + m) % n_j
        for k in range(1, n_y):
            arrived(from_y.at[j, k], ry_recv.at[j, k])
        total = picked[y, j]
        for k in range(1, n_y):
            total = total + from_y[j, k]
        summed[j] = total
        if m:
            to_collector(m).start()
        else:
            pl.when(jnp.logical_not(collects))(lambda: to_collector(0).start())
        if m == j_order[0]:
            pl.when(jnp.logical_and(y == 0, collects))(pass_top_on)

    def along_z(ref, send_sems, recv_sems, k):
        return remote(ref.at[mine], ref.at[mine], send_sems.at[k], recv_sems.at[j_own], y * n_z + z_peer(k), c)

    def spread_z(ref, send_sems, recv_sems):
        for k in near_first(n_z):
            along_z(ref, send_sems, recv_sems, k).start()

    def hand_on(ref, send_sems, recv_sems, m):
        slot = y * n_j + (j_own + m) % n_j
        for k in far_first(n_y)[:-1]:
            send(ref.at[slot], ref.at[slot], send_sems.at[m, k], recv_sems.at[slot], y_peer(k) * n_z + z, c)

    def hand_on_all(ref, z_sems, send_sems, recv_sems, which):
        for m in which:
            j = (j_own + m) % n_j

            def wait(j=j):
                arrived(ref.at[y * n_j + j], z_sems.at[j])

            if m:
                wait()
            else:
                pl.when(jnp.logical_not(collects))(wait)
            hand_on(ref, send_sems, recv_sems, m)

    tile = LANES

    def mask(b, carry):
        span = pl.ds(pl.multiple_of(b * tile, tile), tile)
        row = lax.broadcasted_iota(jnp.int32, (tile, width), 0) + b * tile
        hit = (where == row).astype(jnp.float32)
        left[span, width:2 * width] = hit.astype(bf16)
        hit = jnp.sum(hit, axis=1, keepdims=True)
        hit = jnp.where(jnp.logical_and(is_root, b == 0), 1.0, hit)
        keep = jnp.broadcast_to(1.0 - hit, (tile, LANES)).astype(bf16)
        for g in range(cols // LANES):
            part = pl.ds(g * LANES, LANES)
            held[span, part] = held[span, part] * keep
        return carry

    lax.fori_loop(0, rows // tile, mask, 0)

    @pl.when(collects)
    def _():
        @pl.when(y != 0)
        def _():
            arrived(top_all.at[mine], spread_recv.at[0])

        spread_z(top_all, tz_send, tz_recv)

    small[2].wait()

    @pl.when(collects)
    def _():
        total = summed[j_own]
        for k in near_first(n_z):
            zk = z_peer(k)
            arrived(from_z.at[zk], rz_recv.at[zk])
            total = total + from_z[zk]
        u = jnp.dot(inverse_held[...], total.astype(jnp.float32), precision=lax.Precision.HIGHEST,
                    preferred_element_type=jnp.float32)
        u_all[mine] = u.astype(bf16)
        spread_z(u_all, uz_send, uz_recv)

    hand_on_all(top_all, tz_recv, ty_send, ty_recv, [0, 1])

    for k in range(1, n_c):
        arrived(panels.at[(c + n_c - k) % n_c], panel_recv.at[k])
    whole = jnp.concatenate([panels[k] for k in range(n_c)], axis=0)
    left[:, 0:width] = -whole.astype(jnp.float32).T.astype(bf16)

    @pl.when(is_root)
    def _():
        row = lax.broadcasted_iota(jnp.int32, (width, width), 0)
        col = lax.broadcasted_iota(jnp.int32, (width, width), 1)
        left[0:width, 0:width] = (row == col).astype(bf16)

    hand_on_all(u_all, uz_recv, uy_send, uy_recv, [0])
    hand_on_all(top_all, tz_recv, ty_send, ty_recv, [3])
    hand_on_all(u_all, uz_recv, uy_send, uy_recv, [1])
    hand_on_all(top_all, tz_recv, ty_send, ty_recv, [2])
    hand_on_all(u_all, uz_recv, uy_send, uy_recv, [3, 2])

    finished = len(sent) - 3 * (n_y - 1)
    for copy in sent[:finished]:
        copy.wait_send()
    for m in range(1, n_j):
        to_collector(m).wait_send()
    pl.when(jnp.logical_not(collects))(lambda: to_collector(0).wait_send())

    for first, ref, sems in ((width, top_all, ty_recv), (0, u_all, uy_recv)):
        for k in range(n_y):
            for j in range(n_j):
                slot = y_peer(k) * n_j + j
                if k:
                    arrived(ref.at[slot], sems.at[slot])
                right[first:first + width, pl.ds(pl.multiple_of(slot * LANES, LANES), LANES)] = ref[slot]

    for copy in sent[finished:]:
        copy.wait_send()

    @pl.when(collects)
    def _():
        for k in range(1, n_z):
            along_z(top_all, tz_send, tz_recv, k).wait_send()
            along_z(u_all, uz_send, uz_recv, k).wait_send()

    @pl.when(is_root)
    def _():
        for j in range(1, n_j):
            top_along_z(j).wait_send()

    @pl.when(jnp.logical_and(y == 0, collects))
    def _():
        for k in range(1, n_y):
            top_along_y(k).wait_send()


def update(parts, held, left, right, out_ref, done, sems):
    step = held.shape[1] // parts
    for n in range(parts):
        span = slice(n * step, (n + 1) * step)
        term = jnp.dot(left[...], right[:, span], preferred_element_type=jnp.float32)
        done[n] = (held[:, span].astype(jnp.float32) + term).astype(jnp.bfloat16)
        pltpu.make_async_copy(done.at[n], out_ref.at[:, span], sems.at[n]).start()
    for n in range(parts):
        span = slice(n * step, (n + 1) * step)
        pltpu.make_async_copy(done.at[n], out_ref.at[:, span], sems.at[n]).wait()


def shards(trailing, panel_block, lower_inverse, pivot_pairs):
    rows, cols = trailing.shape
    width = lower_inverse.shape[0]
    procs, n_c = lax.axis_size("prow"), lax.axis_size("pcol")
    n_y, n_z = torus_of(procs)
    n_j, share = n_z // 2, width // n_c
    bf16 = jnp.bfloat16
    dma = pltpu.SemaphoreType.DMA
    vmem = pl.BlockSpec(memory_space=pltpu.VMEM)
    factors = pl.pallas_call(
        functools.partial(kernel, n_y, n_z, n_c, rows, cols, width),
        out_shape=[
            pltpu.VMEM((rows, cols), bf16), pltpu.VMEM((rows, 2 * width), bf16), pltpu.VMEM((2 * width, cols), bf16)
        ],
        in_specs=[pl.BlockSpec(memory_space=pltpu.HBM)] * 4,
        out_specs=[vmem] * 3,
        scratch_shapes=[
            pltpu.VMEM((width, rows), bf16),
            pltpu.VMEM((n_y, n_j, width, LANES), bf16),
            pltpu.VMEM((n_j, n_y, width, LANES), bf16),
            pltpu.VMEM((n_j, width, LANES), bf16),
            pltpu.VMEM((n_z, width, LANES), bf16),
            pltpu.VMEM((n_y * n_j, width, LANES), bf16),
            pltpu.VMEM((n_y * n_j, width, LANES), bf16),
            pltpu.VMEM((n_j, n_y, width, LANES), bf16),
            pltpu.VMEM((n_y, width, LANES), bf16),
            pltpu.VMEM((n_c, share, rows), bf16),
            pltpu.VMEM((share, rows), bf16),
            pltpu.VMEM((width, width), jnp.float32),
            pltpu.VMEM((1, width), jnp.int32),
            dma((3,)), dma((n_y,)), dma((n_j, n_y)), dma((n_j, n_y)), dma((n_j,)), dma((n_z,)),
            dma((n_j,)), dma((1,)), dma((n_y,)), dma((1,)),
            dma((n_z,)), dma((n_j,)), dma((n_j, n_y)), dma((n_y * n_j,)),
            dma((n_z,)), dma((n_j,)), dma((n_j, n_y)), dma((n_y * n_j,)), dma((n_c,)), dma((n_c,)),
        ],
        compiler_params=pltpu.CompilerParams(
            collective_id=0, has_side_effects=True, vmem_limit_bytes=32 * 1024 * 1024
        ),
        name="exchange",
    )(*(
        pltpu.with_memory_space_constraint(value, pltpu.HBM)
        for value in (trailing, panel_block.T, lower_inverse, pivot_pairs.reshape(1, width))
    ))
    parts = cols // (2 * LANES)
    return pl.pallas_call(
        functools.partial(update, parts),
        out_shape=jax.ShapeDtypeStruct((rows, cols), bf16),
        in_specs=[vmem] * 3,
        out_specs=pl.BlockSpec(memory_space=pltpu.HBM),
        scratch_shapes=[pltpu.VMEM((parts, rows, cols // parts), bf16), dma((parts,))],
        compiler_params=pltpu.CompilerParams(vmem_limit_bytes=32 * 1024 * 1024),
        name="update",
    )(*(pltpu.with_memory_space_constraint(value, pltpu.VMEM) for value in factors))


def solution(mesh):
    in_specs = (P("prow", "pcol"), P("prow", "pcol"), P(), P())
    out_specs = P("prow", "pcol")
    return jax.shard_map(shards, mesh=mesh, in_specs=in_specs, out_specs=out_specs, check_vma=False)
```

```python
import functools

import jax
import jax.numpy as jnp
from jax import lax
from jax.experimental import pallas as pl
from jax.experimental.pallas import tpu as pltpu
from jax.sharding import PartitionSpec as P

MESH = pl.DeviceIdType.MESH
LANES = 128


def torus_of(procs):
    n_y = {32: 4, 8: 2}[procs]
    return n_y, procs // n_y


def near_first(n):
    return sorted(range(1, n), key=lambda k: (min(k, n - k), k))


def far_first(n):
    return sorted(range(n), key=lambda k: (-min(k, n - k), k))


def kernel(n_y, n_z, n_c, rows, cols, width,
           trailing_ref, panel_ref, inverse_ref, pivots_ref, held, left, right,
           select, picked, from_y, summed, from_z, u_all, top_all, top_out, top_in, panels,
           panel_held, inverse_held, pivots_held,
           small_sem, load_sem, ry_send, ry_recv, rz_send, rz_recv, top_send, top_recv, spread_send, spread_recv,
           uz_send, uz_recv, uy_send, uy_recv, tz_send, tz_recv, ty_send, ty_recv, panel_send, panel_recv):
    procs = n_y * n_z
    n_j = n_z // 2
    group = cols // n_y
    share = width // n_c
    me = lax.axis_index("prow")
    c = lax.axis_index("pcol")
    y, z = me // n_z, me % n_z
    j_own, collects = z // 2, z % 2 == 0
    mine = y * n_j + j_own
    is_root = me == 0
    bf16 = jnp.bfloat16

    def y_peer(k):
        return (y + k) % n_y

    def z_peer(k):
        return (z + k) % n_z

    def remote(src, dst, send_sem, recv_sem, row, col):
        return pltpu.make_async_remote_copy(
            src_ref=src, dst_ref=dst, send_sem=send_sem, recv_sem=recv_sem,
            device_id=(row, col), device_id_type=MESH,
        )

    sent = []

    def send(*what):
        copy = remote(*what)
        copy.start()
        sent.append(copy)

    def arrived(dst, recv_sem):
        remote(dst, dst, recv_sem, recv_sem, me, c).wait_recv()

    barrier = pltpu.get_barrier_semaphore()
    for k in far_first(n_z)[:-1]:
        pl.semaphore_signal(barrier, inc=1, device_id=(y * n_z + z_peer(k), c), device_id_type=MESH)
    for k in far_first(n_y)[:-1]:
        pl.semaphore_signal(barrier, inc=1, device_id=(y_peer(k) * n_z + z, c), device_id_type=MESH)
    for k in range(1, n_c):
        pl.semaphore_signal(barrier, inc=1, device_id=(me, (c + k) % n_c), device_id_type=MESH)

    small = [
        pltpu.make_async_copy(pivots_ref, pivots_held, small_sem.at[0]),
        pltpu.make_async_copy(panel_ref, panel_held, small_sem.at[1]),
        pltpu.make_async_copy(inverse_ref, inverse_held, small_sem.at[2]),
    ]
    small[0].start()

    y_order = far_first(n_y)
    loads = []
    for k in y_order:
        span = pl.ds(pl.multiple_of(y_peer(k) * group, group), group)
        load = pltpu.make_async_copy(trailing_ref.at[:, span], held.at[:, span], load_sem.at[k])
        load.start()
        loads.append(load)
    small[1].start()
    small[2].start()

    small[0].wait()
    pivots = pivots_held[...]
    block = pivots // width
    where = jnp.where(block % procs == me, block // procs * width + pivots % width, -1)
    spread = jnp.broadcast_to(where.astype(jnp.float32), (width, width)).T
    for b in range(rows // LANES):
        row = lax.broadcasted_iota(jnp.int32, (width, LANES), 1) + b * LANES
        select[:, b * LANES:(b + 1) * LANES] = (spread == row.astype(jnp.float32)).astype(bf16)

    j_order = far_first(n_j)
    for n, k in enumerate(y_order):
        loads[n].wait()
        yk = y_peer(k)
        span = pl.ds(pl.multiple_of(yk * group, group), group)
        found = jnp.dot(select[...], held[:, span], preferred_element_type=jnp.float32).astype(bf16)
        for j in range(n_j):
            picked[yk, j] = found[:, j * LANES:(j + 1) * LANES]

    @pl.when(is_root)
    def _():
        for j in far_first(n_j):
            for q in range(n_y):
                at = (q * n_j + j) * LANES
                top_out[j, q] = held[0:width, at:at + LANES]
        top_in[...] = top_out[0]

    pl.semaphore_wait(barrier, n_y - 1 + n_z - 1 + n_c - 1)

    def top_along_z(j):
        return remote(top_out.at[j], top_in, top_send.at[j], top_recv.at[0], j * 2, c)

    @pl.when(is_root)
    def _():
        for j in far_first(n_j)[:-1]:
            top_along_z(j).start()

    for m in j_order:
        j = (j_own + m) % n_j
        for k in far_first(n_y)[:-1]:
            yk = y_peer(k)
            send(picked.at[yk, j], from_y.at[j, k], ry_send.at[m, k], ry_recv.at[j, k], yk * n_z + z, c)

    small[1].wait()
    for k in range(1, n_c):
        ck = (c + k) % n_c
        send(panel_held, panels.at[c], panel_send.at[k], panel_recv.at[k], me, ck)
    panels[c] = panel_held[...]

    def top_along_y(k):
        return remote(top_in.at[k], top_all.at[k * n_j + j_own], spread_send.at[k], spread_recv.at[0],
                      k * n_z + z, c)

    def pass_top_on():
        @pl.when(z != 0)
        def _():
            arrived(top_in, top_recv.at[0])
        for k in far_first(n_y)[:-1]:
            top_along_y(k).start()
        top_all[mine] = top_in[0]

    pl.when(jnp.logical_and(y == 0, collects))(pass_top_on)

    def to_collector(m):
        j = (j_own + m) % n_j
        return remote(summed.at[j], from_z.at[z], rz_send.at[m], rz_recv.at[z], y * n_z + j * 2, c)

    for m in j_order:
        j = (j_own + m) % n_j
        for k in range(1, n_y):
            arrived(from_y.at[j, k], ry_recv.at[j, k])
        total = picked[y, j]
        for k in range(1, n_y):
            total = total + from_y[j, k]
        summed[j] = total
        if m:
            to_collector(m).start()
        else:
            pl.when(jnp.logical_not(collects))(lambda: to_collector(0).start())

    def along_z(ref, send_sems, recv_sems, k):
        return remote(ref.at[mine], ref.at[mine], send_sems.at[k], recv_sems.at[j_own], y * n_z + z_peer(k), c)

    def spread_z(ref, send_sems, recv_sems):
        for k in near_first(n_z):
            along_z(ref, send_sems, recv_sems, k).start()

    def hand_on(ref, send_sems, recv_sems, m):
        slot = y * n_j + (j_own + m) % n_j
        for k in far_first(n_y)[:-1]:
            send(ref.at[slot], ref.at[slot], send_sems.at[m, k], recv_sems.at[slot], y_peer(k) * n_z + z, c)

    def hand_on_all(ref, z_sems, send_sems, recv_sems, which):
        for m in which:
            j = (j_own + m) % n_j

            def wait(j=j):
                arrived(ref.at[y * n_j + j], z_sems.at[j])

            if m:
                wait()
            else:
                pl.when(jnp.logical_not(collects))(wait)
            hand_on(ref, send_sems, recv_sems, m)

    @pl.when(collects)
    def _():
        @pl.when(y != 0)
        def _():
            arrived(top_all.at[mine], spread_recv.at[0])

        spread_z(top_all, tz_send, tz_recv)

    tile = LANES

    def mask(b, carry):
        span = pl.ds(pl.multiple_of(b * tile, tile), tile)
        row = lax.broadcasted_iota(jnp.int32, (tile, width), 0) + b * tile
        hit = (where == row).astype(jnp.float32)
        left[span, width:2 * width] = hit.astype(bf16)
        hit = jnp.sum(hit, axis=1, keepdims=True)
        hit = jnp.where(jnp.logical_and(is_root, b == 0), 1.0, hit)
        keep = jnp.broadcast_to(1.0 - hit, (tile, LANES)).astype(bf16)
        for g in range(cols // LANES):
            part = pl.ds(g * LANES, LANES)
            held[span, part] = held[span, part] * keep
        return carry

    lax.fori_loop(0, rows // tile, mask, 0)

    small[2].wait()

    @pl.when(collects)
    def _():
        total = summed[j_own]
        for k in near_first(n_z):
            zk = z_peer(k)
            arrived(from_z.at[zk], rz_recv.at[zk])
            total = total + from_z[zk]
        u = jnp.dot(inverse_held[...], total.astype(jnp.float32), precision=lax.Precision.HIGHEST,
                    preferred_element_type=jnp.float32)
        u_all[mine] = u.astype(bf16)
        spread_z(u_all, uz_send, uz_recv)

    hand_on_all(top_all, tz_recv, ty_send, ty_recv, [0, 1])

    for k in range(1, n_c):
        arrived(panels.at[(c + n_c - k) % n_c], panel_recv.at[k])
    whole = jnp.concatenate([panels[k] for k in range(n_c)], axis=0)
    left[:, 0:width] = -whole.astype(jnp.float32).T.astype(bf16)

    @pl.when(is_root)
    def _():
        row = lax.broadcasted_iota(jnp.int32, (width, width), 0)
        col = lax.broadcasted_iota(jnp.int32, (width, width), 1)
        left[0:width, 0:width] = (row == col).astype(bf16)

    hand_on_all(u_all, uz_recv, uy_send, uy_recv, [0])
    hand_on_all(top_all, tz_recv, ty_send, ty_recv, [3])
    hand_on_all(u_all, uz_recv, uy_send, uy_recv, [1])
    hand_on_all(top_all, tz_recv, ty_send, ty_recv, [2])
    hand_on_all(u_all, uz_recv, uy_send, uy_recv, [3, 2])

    finished = len(sent) - 3 * (n_y - 1)
    for copy in sent[:finished]:
        copy.wait_send()
    for m in range(1, n_j):
        to_collector(m).wait_send()
    pl.when(jnp.logical_not(collects))(lambda: to_collector(0).wait_send())

    for first, ref, sems in ((width, top_all, ty_recv), (0, u_all, uy_recv)):
        for k in range(n_y):
            for j in range(n_j):
                slot = y_peer(k) * n_j + j
                if k:
                    arrived(ref.at[slot], sems.at[slot])
                right[first:first + width, pl.ds(pl.multiple_of(slot * LANES, LANES), LANES)] = ref[slot]

    for copy in sent[finished:]:
        copy.wait_send()

    @pl.when(collects)
    def _():
        for k in range(1, n_z):
            along_z(top_all, tz_send, tz_recv, k).wait_send()
            along_z(u_all, uz_send, uz_recv, k).wait_send()

    @pl.when(is_root)
    def _():
        for j in range(1, n_j):
            top_along_z(j).wait_send()

    @pl.when(jnp.logical_and(y == 0, collects))
    def _():
        for k in range(1, n_y):
            top_along_y(k).wait_send()


def update(parts, held, left, right, out_ref, done, sems):
    step = held.shape[0] // parts
    for n in range(parts):
        span = slice(n * step, (n + 1) * step)
        term = jnp.dot(left[span, :], right[...], preferred_element_type=jnp.float32)
        done[n] = (held[span, :].astype(jnp.float32) + term).astype(jnp.bfloat16)
        pltpu.make_async_copy(done.at[n], out_ref.at[span, :], sems.at[n]).start()
    for n in range(parts):
        span = slice(n * step, (n + 1) * step)
        pltpu.make_async_copy(done.at[n], out_ref.at[span, :], sems.at[n]).wait()


def shards(trailing, panel_block, lower_inverse, pivot_pairs):
    rows, cols = trailing.shape
    width = lower_inverse.shape[0]
    procs, n_c = lax.axis_size("prow"), lax.axis_size("pcol")
    n_y, n_z = torus_of(procs)
    n_j, share = n_z // 2, width // n_c
    bf16 = jnp.bfloat16
    dma = pltpu.SemaphoreType.DMA
    vmem = pl.BlockSpec(memory_space=pltpu.VMEM)
    factors = pl.pallas_call(
        functools.partial(kernel, n_y, n_z, n_c, rows, cols, width),
        out_shape=[
            pltpu.VMEM((rows, cols), bf16), pltpu.VMEM((rows, 2 * width), bf16), pltpu.VMEM((2 * width, cols), bf16)
        ],
        in_specs=[pl.BlockSpec(memory_space=pltpu.HBM)] * 4,
        out_specs=[vmem] * 3,
        scratch_shapes=[
            pltpu.VMEM((width, rows), bf16),
            pltpu.VMEM((n_y, n_j, width, LANES), bf16),
            pltpu.VMEM((n_j, n_y, width, LANES), bf16),
            pltpu.VMEM((n_j, width, LANES), bf16),
            pltpu.VMEM((n_z, width, LANES), bf16),
            pltpu.VMEM((n_y * n_j, width, LANES), bf16),
            pltpu.VMEM((n_y * n_j, width, LANES), bf16),
            pltpu.VMEM((n_j, n_y, width, LANES), bf16),
            pltpu.VMEM((n_y, width, LANES), bf16),
            pltpu.VMEM((n_c, share, rows), bf16),
            pltpu.VMEM((share, rows), bf16),
            pltpu.VMEM((width, width), jnp.float32),
            pltpu.VMEM((1, width), jnp.int32),
            dma((3,)), dma((n_y,)), dma((n_j, n_y)), dma((n_j, n_y)), dma((n_j,)), dma((n_z,)),
            dma((n_j,)), dma((1,)), dma((n_y,)), dma((1,)),
            dma((n_z,)), dma((n_j,)), dma((n_j, n_y)), dma((n_y * n_j,)),
            dma((n_z,)), dma((n_j,)), dma((n_j, n_y)), dma((n_y * n_j,)), dma((n_c,)), dma((n_c,)),
        ],
        compiler_params=pltpu.CompilerParams(
            collective_id=0, has_side_effects=True, vmem_limit_bytes=32 * 1024 * 1024
        ),
        name="exchange",
    )(*(
        pltpu.with_memory_space_constraint(value, pltpu.HBM)
        for value in (trailing, panel_block.T, lower_inverse, pivot_pairs.reshape(1, width))
    ))
    parts = cols // (2 * LANES)
    return pl.pallas_call(
        functools.partial(update, parts),
        out_shape=jax.ShapeDtypeStruct((rows, cols), bf16),
        in_specs=[vmem] * 3,
        out_specs=pl.BlockSpec(memory_space=pltpu.HBM),
        scratch_shapes=[pltpu.VMEM((parts, rows // parts, cols), bf16), dma((parts,))],
        compiler_params=pltpu.CompilerParams(vmem_limit_bytes=32 * 1024 * 1024),
        name="update",
    )(*(pltpu.with_memory_space_constraint(value, pltpu.VMEM) for value in factors))


def solution(mesh):
    in_specs = (P("prow", "pcol"), P("prow", "pcol"), P(), P())
    out_specs = P("prow", "pcol")
    return jax.shard_map(shards, mesh=mesh, in_specs=in_specs, out_specs=out_specs, check_vma=False)
```

```python
import functools

import jax
import jax.numpy as jnp
from jax import lax
from jax.experimental import pallas as pl
from jax.experimental.pallas import tpu as pltpu
from jax.sharding import PartitionSpec as P

MESH = pl.DeviceIdType.MESH
LANES = 128


def torus_of(procs):
    n_y = {32: 4, 8: 2}[procs]
    return n_y, procs // n_y


def near_first(n):
    return sorted(range(1, n), key=lambda k: (min(k, n - k), k))


def far_first(n):
    return sorted(range(n), key=lambda k: (-min(k, n - k), k))


def kernel(n_y, n_z, n_c, rows, cols, width,
           trailing_ref, panel_ref, inverse_ref, pivots_ref, held, left, right,
           select, picked, from_y, summed, from_z, u_all, top_all, top_out, top_in, panels,
           panel_held, inverse_held, pivots_held,
           small_sem, load_sem, ry_send, ry_recv, rz_send, rz_recv, top_send, top_recv, spread_send, spread_recv,
           uz_send, uz_recv, uy_send, uy_recv, tz_send, tz_recv, ty_send, ty_recv, panel_send, panel_recv):
    procs = n_y * n_z
    n_j = n_z // 2
    group = cols // n_y
    share = width // n_c
    me = lax.axis_index("prow")
    c = lax.axis_index("pcol")
    y, z = me // n_z, me % n_z
    j_own, collects = z // 2, z % 2 == 0
    mine = y * n_j + j_own
    is_root = me == 0
    bf16 = jnp.bfloat16

    def y_peer(k):
        return (y + k) % n_y

    def z_peer(k):
        return (z + k) % n_z

    def remote(src, dst, send_sem, recv_sem, row, col):
        return pltpu.make_async_remote_copy(
            src_ref=src, dst_ref=dst, send_sem=send_sem, recv_sem=recv_sem,
            device_id=(row, col), device_id_type=MESH,
        )

    sent = []

    def send(*what):
        copy = remote(*what)
        copy.start()
        sent.append(copy)

    def arrived(dst, recv_sem):
        remote(dst, dst, recv_sem, recv_sem, me, c).wait_recv()

    barrier = pltpu.get_barrier_semaphore()
    for k in far_first(n_z)[:-1]:
        pl.semaphore_signal(barrier, inc=1, device_id=(y * n_z + z_peer(k), c), device_id_type=MESH)
    for k in far_first(n_y)[:-1]:
        pl.semaphore_signal(barrier, inc=1, device_id=(y_peer(k) * n_z + z, c), device_id_type=MESH)
    for k in range(1, n_c):
        pl.semaphore_signal(barrier, inc=1, device_id=(me, (c + k) % n_c), device_id_type=MESH)

    small = [
        pltpu.make_async_copy(pivots_ref, pivots_held, small_sem.at[0]),
        pltpu.make_async_copy(panel_ref, panel_held, small_sem.at[1]),
        pltpu.make_async_copy(inverse_ref, inverse_held, small_sem.at[2]),
    ]
    small[0].start()

    y_order = far_first(n_y)
    loads = []
    for k in y_order:
        span = pl.ds(pl.multiple_of(y_peer(k) * group, group), group)
        load = pltpu.make_async_copy(trailing_ref.at[:, span], held.at[:, span], load_sem.at[k])
        load.start()
        loads.append(load)
    small[1].start()
    small[2].start()

    small[0].wait()
    pivots = pivots_held[...]
    block = pivots // width
    where = jnp.where(block % procs == me, block // procs * width + pivots % width, -1)
    spread = jnp.broadcast_to(where.astype(jnp.float32), (width, width)).T
    for b in range(rows // LANES):
        row = lax.broadcasted_iota(jnp.int32, (width, LANES), 1) + b * LANES
        select[:, b * LANES:(b + 1) * LANES] = (spread == row.astype(jnp.float32)).astype(bf16)

    j_order = far_first(n_j)
    for n, k in enumerate(y_order):
        loads[n].wait()
        yk = y_peer(k)
        span = pl.ds(pl.multiple_of(yk * group, group), group)
        found = jnp.dot(select[...], held[:, span], preferred_element_type=jnp.float32).astype(bf16)
        for j in range(n_j):
            picked[yk, j] = found[:, j * LANES:(j + 1) * LANES]

    @pl.when(is_root)
    def _():
        for j in far_first(n_j):
            for q in range(n_y):
                at = (q * n_j + j) * LANES
                top_out[j, q] = held[0:width, at:at + LANES]
        top_in[...] = top_out[0]

    pl.semaphore_wait(barrier, n_y - 1 + n_z - 1 + n_c - 1)

    def top_along_z(j):
        return remote(top_out.at[j], top_in, top_send.at[j], top_recv.at[0], j * 2, c)

    @pl.when(is_root)
    def _():
        for j in far_first(n_j)[:-1]:
            top_along_z(j).start()

    for m in j_order:
        j = (j_own + m) % n_j
        for k in far_first(n_y)[:-1]:
            yk = y_peer(k)
            send(picked.at[yk, j], from_y.at[j, k], ry_send.at[m, k], ry_recv.at[j, k], yk * n_z + z, c)

    small[1].wait()
    for k in range(1, n_c):
        ck = (c + k) % n_c
        send(panel_held, panels.at[c], panel_send.at[k], panel_recv.at[k], me, ck)
    panels[c] = panel_held[...]

    def top_along_y(k):
        return remote(top_in.at[k], top_all.at[k * n_j + j_own], spread_send.at[k], spread_recv.at[0],
                      k * n_z + z, c)

    def pass_top_on():
        @pl.when(z != 0)
        def _():
            arrived(top_in, top_recv.at[0])
        for k in far_first(n_y)[:-1]:
            top_along_y(k).start()
        top_all[mine] = top_in[0]

    pl.when(jnp.logical_and(y == 0, collects))(pass_top_on)

    def to_collector(m):
        j = (j_own + m) % n_j
        return remote(summed.at[j], from_z.at[z], rz_send.at[m], rz_recv.at[z], y * n_z + j * 2, c)

    for m in j_order:
        j = (j_own + m) % n_j
        for k in range(1, n_y):
            arrived(from_y.at[j, k], ry_recv.at[j, k])
        total = picked[y, j]
        for k in range(1, n_y):
            total = total + from_y[j, k]
        summed[j] = total
        if m:
            to_collector(m).start()
        else:
            pl.when(jnp.logical_not(collects))(lambda: to_collector(0).start())

    def along_z(ref, send_sems, recv_sems, k):
        return remote(ref.at[mine], ref.at[mine], send_sems.at[k], recv_sems.at[j_own], y * n_z + z_peer(k), c)

    def spread_z(ref, send_sems, recv_sems):
        for k in near_first(n_z):
            along_z(ref, send_sems, recv_sems, k).start()

    def hand_on(ref, send_sems, recv_sems, m):
        slot = y * n_j + (j_own + m) % n_j
        for k in far_first(n_y)[:-1]:
            send(ref.at[slot], ref.at[slot], send_sems.at[m, k], recv_sems.at[slot], y_peer(k) * n_z + z, c)

    def hand_on_all(ref, z_sems, send_sems, recv_sems, which):
        for m in which:
            j = (j_own + m) % n_j

            def wait(j=j):
                arrived(ref.at[y * n_j + j], z_sems.at[j])

            if m:
                wait()
            else:
                pl.when(jnp.logical_not(collects))(wait)
            hand_on(ref, send_sems, recv_sems, m)

    @pl.when(collects)
    def _():
        @pl.when(y != 0)
        def _():
            arrived(top_all.at[mine], spread_recv.at[0])

        spread_z(top_all, tz_send, tz_recv)

    tile = LANES

    def mask(b, carry):
        span = pl.ds(pl.multiple_of(b * tile, tile), tile)
        row = lax.broadcasted_iota(jnp.int32, (tile, width), 0) + b * tile
        hit = (where == row).astype(jnp.float32)
        left[span, width:2 * width] = hit.astype(bf16)
        hit = jnp.sum(hit, axis=1, keepdims=True)
        hit = jnp.where(jnp.logical_and(is_root, b == 0), 1.0, hit)
        keep = jnp.broadcast_to(1.0 - hit, (tile, LANES)).astype(bf16)
        for g in range(cols // LANES):
            part = pl.ds(g * LANES, LANES)
            held[span, part] = held[span, part] * keep
        return carry

    lax.fori_loop(0, rows // tile, mask, 0)

    hand_on_all(top_all, tz_recv, ty_send, ty_recv, [0])

    small[2].wait()

    @pl.when(collects)
    def _():
        total = summed[j_own]
        for k in near_first(n_z):
            zk = z_peer(k)
            arrived(from_z.at[zk], rz_recv.at[zk])
            total = total + from_z[zk]
        u = jnp.dot(inverse_held[...], total.astype(jnp.float32), precision=lax.Precision.HIGHEST,
                    preferred_element_type=jnp.float32)
        u_all[mine] = u.astype(bf16)
        spread_z(u_all, uz_send, uz_recv)

    hand_on_all(top_all, tz_recv, ty_send, ty_recv, [1, 3])

    for k in range(1, n_c):
        arrived(panels.at[(c + n_c - k) % n_c], panel_recv.at[k])
    whole = jnp.concatenate([panels[k] for k in range(n_c)], axis=0)
    left[:, 0:width] = -whole.astype(jnp.float32).T.astype(bf16)

    @pl.when(is_root)
    def _():
        row = lax.broadcasted_iota(jnp.int32, (width, width), 0)
        col = lax.broadcasted_iota(jnp.int32, (width, width), 1)
        left[0:width, 0:width] = (row == col).astype(bf16)

    hand_on_all(u_all, uz_recv, uy_send, uy_recv, [0])
    hand_on_all(u_all, uz_recv, uy_send, uy_recv, [1])
    hand_on_all(top_all, tz_recv, ty_send, ty_recv, [2])
    hand_on_all(u_all, uz_recv, uy_send, uy_recv, [3, 2])

    finished = len(sent) - 3 * (n_y - 1)
    for copy in sent[:finished]:
        copy.wait_send()
    for m in range(1, n_j):
        to_collector(m).wait_send()
    pl.when(jnp.logical_not(collects))(lambda: to_collector(0).wait_send())

    for first, ref, sems in ((width, top_all, ty_recv), (0, u_all, uy_recv)):
        for k in range(n_y):
            for j in range(n_j):
                slot = y_peer(k) * n_j + j
                if k:
                    arrived(ref.at[slot], sems.at[slot])
                right[first:first + width, pl.ds(pl.multiple_of(slot * LANES, LANES), LANES)] = ref[slot]

    for copy in sent[finished:]:
        copy.wait_send()

    @pl.when(collects)
    def _():
        for k in range(1, n_z):
            along_z(top_all, tz_send, tz_recv, k).wait_send()
            along_z(u_all, uz_send, uz_recv, k).wait_send()

    @pl.when(is_root)
    def _():
        for j in range(1, n_j):
            top_along_z(j).wait_send()

    @pl.when(jnp.logical_and(y == 0, collects))
    def _():
        for k in range(1, n_y):
            top_along_y(k).wait_send()


def update(parts, held, left, right, out_ref, done, sems):
    step = held.shape[0] // parts
    for n in range(parts):
        span = slice(n * step, (n + 1) * step)
        term = jnp.dot(left[span, :], right[...], preferred_element_type=jnp.float32)
        done[n] = (held[span, :].astype(jnp.float32) + term).astype(jnp.bfloat16)
        pltpu.make_async_copy(done.at[n], out_ref.at[span, :], sems.at[n]).start()
    for n in range(parts):
        span = slice(n * step, (n + 1) * step)
        pltpu.make_async_copy(done.at[n], out_ref.at[span, :], sems.at[n]).wait()


def shards(trailing, panel_block, lower_inverse, pivot_pairs):
    rows, cols = trailing.shape
    width = lower_inverse.shape[0]
    procs, n_c = lax.axis_size("prow"), lax.axis_size("pcol")
    n_y, n_z = torus_of(procs)
    n_j, share = n_z // 2, width // n_c
    bf16 = jnp.bfloat16
    dma = pltpu.SemaphoreType.DMA
    vmem = pl.BlockSpec(memory_space=pltpu.VMEM)
    factors = pl.pallas_call(
        functools.partial(kernel, n_y, n_z, n_c, rows, cols, width),
        out_shape=[
            pltpu.VMEM((rows, cols), bf16), pltpu.VMEM((rows, 2 * width), bf16), pltpu.VMEM((2 * width, cols), bf16)
        ],
        in_specs=[pl.BlockSpec(memory_space=pltpu.HBM)] * 4,
        out_specs=[vmem] * 3,
        scratch_shapes=[
            pltpu.VMEM((width, rows), bf16),
            pltpu.VMEM((n_y, n_j, width, LANES), bf16),
            pltpu.VMEM((n_j, n_y, width, LANES), bf16),
            pltpu.VMEM((n_j, width, LANES), bf16),
            pltpu.VMEM((n_z, width, LANES), bf16),
            pltpu.VMEM((n_y * n_j, width, LANES), bf16),
            pltpu.VMEM((n_y * n_j, width, LANES), bf16),
            pltpu.VMEM((n_j, n_y, width, LANES), bf16),
            pltpu.VMEM((n_y, width, LANES), bf16),
            pltpu.VMEM((n_c, share, rows), bf16),
            pltpu.VMEM((share, rows), bf16),
            pltpu.VMEM((width, width), jnp.float32),
            pltpu.VMEM((1, width), jnp.int32),
            dma((3,)), dma((n_y,)), dma((n_j, n_y)), dma((n_j, n_y)), dma((n_j,)), dma((n_z,)),
            dma((n_j,)), dma((1,)), dma((n_y,)), dma((1,)),
            dma((n_z,)), dma((n_j,)), dma((n_j, n_y)), dma((n_y * n_j,)),
            dma((n_z,)), dma((n_j,)), dma((n_j, n_y)), dma((n_y * n_j,)), dma((n_c,)), dma((n_c,)),
        ],
        compiler_params=pltpu.CompilerParams(
            collective_id=0, has_side_effects=True, vmem_limit_bytes=32 * 1024 * 1024
        ),
        name="exchange",
    )(*(
        pltpu.with_memory_space_constraint(value, pltpu.HBM)
        for value in (trailing, panel_block.T, lower_inverse, pivot_pairs.reshape(1, width))
    ))
    parts = cols // (2 * LANES)
    return pl.pallas_call(
        functools.partial(update, parts),
        out_shape=jax.ShapeDtypeStruct((rows, cols), bf16),
        in_specs=[vmem] * 3,
        out_specs=pl.BlockSpec(memory_space=pltpu.HBM),
        scratch_shapes=[pltpu.VMEM((parts, rows // parts, cols), bf16), dma((parts,))],
        compiler_params=pltpu.CompilerParams(vmem_limit_bytes=32 * 1024 * 1024),
        name="update",
    )(*(pltpu.with_memory_space_constraint(value, pltpu.VMEM) for value in factors))


def solution(mesh):
    in_specs = (P("prow", "pcol"), P("prow", "pcol"), P(), P())
    out_specs = P("prow", "pcol")
    return jax.shard_map(shards, mesh=mesh, in_specs=in_specs, out_specs=out_specs, check_vma=False)
```
